32 devices in a mesh: dp: 32 (over z, y, x, core).
Axes of the slice: x: 2, y: 2, z: 4, core: 2. Of those that a mesh axis runs over, the one named last changes fastest.
Arguments:
- tokens: bfloat16 [32768, 768], P('dp'), may hold values from -6 to 6
- segment: int32 [32768], P('dp'), may hold values from -1 to 4, as said below
- ln1_gain: bfloat16 [768], P('dp'), may hold values from 0.099609375 to 1.8984375
- ln1_bias: bfloat16 [768], P('dp'), may hold values from -3 to 3
- w_qkv: bfloat16 [768, 2304], P('dp'), may hold values from -0.21875 to 0.21875
- b_query: bfloat16 [768], P('dp'), may hold values from -3 to 3
- b_value: bfloat16 [768], P('dp'), may hold values from -3 to 3
- w_out: bfloat16 [768, 768], P('dp'), may hold values from -3.5 to 3.5
- b_out: bfloat16 [768], P('dp'), may hold values from -3 to 3
- ln2_gain: bfloat16 [768], P('dp'), may hold values from 0.099609375 to 1.8984375
- ln2_bias: bfloat16 [768], P('dp'), may hold values from -3 to 3
- w_up: bfloat16 [768, 3072], P('dp'), may hold values from -0.21875 to 0.21875
- b_up: bfloat16 [3072], P('dp'), may hold values from -3 to 3
- w_down: bfloat16 [3072, 768], P('dp'), may hold values from -0.109375 to 0.109375
- b_down: bfloat16 [768], P('dp'), may hold values from -3 to 3
- cotangent: bfloat16 [32768, 768], P('dp'), may hold values from -6 to 6
Outputs:
- block_out: bfloat16 [32768, 768], P('dp')
- grad_tokens: bfloat16 [32768, 768], P('dp')
- grad_ln1_gain: float32 [768], P('dp')
- grad_ln1_bias: float32 [768], P('dp')
- grad_w_qkv: float32 [768, 2304], P('dp')
- grad_b_query: float32 [768], P('dp')
- grad_b_value: float32 [768], P('dp')
- grad_w_out: float32 [768, 768], P('dp')
- grad_b_out: float32 [768], P('dp')
- grad_ln2_gain: float32 [768], P('dp')
- grad_ln2_bias: float32 [768], P('dp')
- grad_w_up: float32 [768, 3072], P('dp')
- grad_b_up: float32 [3072], P('dp')
- grad_w_down: float32 [3072, 768], P('dp')
- grad_b_down: float32 [768], P('dp')
The draws below stay inside these ranges and needn't reach their ends.
Inputs may be any that keep to these rules, and one draw needn't show every extreme that they name: `segment`: each device's 1024 rows hold whole sequences, each of 196 rows (a clip) or 314 rows (a video), labelled 0, 1, 2, ... in row order, then -1 on the rows left over; no sequence crosses devices.
All inputs are finite; a program needn't handle non-finite values.
Results may differ from the reference program's by a relative error of at most 0.012.
Values may be sent and summed in bfloat16 or wider, within the bound.
No kernel may reach another device: no remote copies, remote signals or barrier semaphores. Data moves between devices by JAX's collectives and lax.ppermute only.
A program may use at most 192 MiB of HBM per device.

```python
import jax
import jax.numpy as jnp
from jax import lax

D = 768
HEADS = 12
HEAD_DIM = 64
FF = 3072
ROWS_DEV = 1024
CLIP_LEN = 196
VID_LEN = 314
TOKENS = 32768


def draw_segment(key, part):
    key = jax.random.fold_in(key, 7)
    device_count = TOKENS // ROWS_DEV
    slot_count = ROWS_DEV // CLIP_LEN + 1
    choose_kind = jax.random.randint(key, (device_count, slot_count), 0, 2).astype(jnp.int32)
    later_device = (jnp.arange(device_count).astype(jnp.int32) > 0).astype(jnp.int32)
    choose_kind = choose_kind * later_device[:, None]
    lengths = jnp.where(choose_kind == 1, VID_LEN, CLIP_LEN).astype(jnp.int32)
    seq_ends = jnp.cumsum(lengths, axis=1).astype(jnp.int32)
    row_index = jnp.arange(ROWS_DEV).astype(jnp.int32)
    seq_number = jnp.sum((seq_ends[:, None, :] <= row_index[None, :, None]).astype(jnp.int32), -1)
    whole_count = jnp.sum((seq_ends <= ROWS_DEV).astype(jnp.int32), -1, keepdims=True)
    labels = jnp.where(seq_number < whole_count, seq_number, -1)
    return labels.reshape(-1).astype(jnp.int32)


def block_scale(own_key, extent, pieces, least, high):
    gain, own = 1.0, jax.random.fold_in(own_key, 6)
    for axis_at, blocks in pieces:
        steps = jnp.exp(jax.random.uniform(jax.random.fold_in(own, axis_at), (blocks,), jnp.float32, least / len(pieces), high / len(pieces)))
        gain = gain * jnp.repeat(steps, extent[axis_at] // blocks).reshape([-1 if axis == axis_at else 1 for axis in range(len(extent))])
    return gain


def noise(stream_key, shape, scale, bound, split=(), held_as=jnp.bfloat16):
    factor_of = block_scale(stream_key, shape, split, -0.22, 0.18) if split else 1.0
    values = jax.random.normal(stream_key, shape, jnp.float32) * scale * factor_of
    return jnp.minimum(jnp.maximum(values, -bound), bound).astype(held_as)


def setup_inputs(seed: int = 0) -> dict:
    keys = jax.random.split(jax.random.key(seed), 17)
    return {
        "tokens": noise(keys[0], (TOKENS, D), 1.0, 6.0, ((0, 32),)),
        "segment": draw_segment(jax.random.fold_in(keys[16], 71), 0),
        "ln1_gain": jnp.clip(1.0 + 0.18 * jax.random.normal(keys[2], (D,), jnp.float32), 0.099609375, 1.8984375).astype(jnp.bfloat16),
        "ln1_bias": noise(keys[3], (D,), 0.5, 3.0, ((0, 32),)),
        "w_qkv": noise(keys[4], (D, 3 * D), D ** -0.5, 0.21875, ((0, 32),)),
        "b_query": noise(keys[5], (D,), 0.5, 3.0, ((0, 32),)),
        "b_value": noise(keys[6], (D,), 0.5, 3.0, ((0, 32),)),
        "w_out": noise(keys[7], (D, D), (D // 256) ** -0.5, 3.5, ((0, 32),)),
        "b_out": noise(keys[8], (D,), 0.5, 3.0, ((0, 32),)),
        "ln2_gain": jnp.clip(1.0 + 0.18 * jax.random.normal(keys[9], (D,), jnp.float32), 0.099609375, 1.8984375).astype(jnp.bfloat16),
        "ln2_bias": noise(keys[10], (D,), 0.5, 3.0, ((0, 32),)),
        "w_up": noise(keys[11], (D, FF), D ** -0.5, 0.21875, ((0, 32),)),
        "b_up": noise(keys[12], (FF,), 0.5, 3.0, ((0, 32),)),
        "w_down": noise(keys[13], (FF, D), FF ** -0.5, 0.109375, ((0, 32),)),
        "b_down": noise(keys[14], (D,), 0.5, 3.0, ((0, 32),)),
        "cotangent": noise(keys[15], (TOKENS, D), 1.0, 6.0, ((0, 32),)),
    }


EPSILON = 1e-06
NEGATIVE = -1000000000.0
PRECISE = lax.Precision.HIGHEST

@jax.custom_vjp
def low(v):
    return lax.optimization_barrier(v.astype(jnp.bfloat16)).astype(jnp.float32)

@jax.custom_vjp
def low_back(v):
    return v

def low_keep(v):
    return (low(v), None)

def low_pass(kept, grad):
    return (grad,)

def back_keep(v):
    return (v, None)

def back_low(kept, grad):
    return (low(grad),)
low.defvjp(low_keep, low_pass)
low_back.defvjp(back_keep, back_low)

def layer_norm(values, scale_gain, offset):
    center = values - lax.optimization_barrier(jnp.mean(values, -1, keepdims=True))
    spread = lax.optimization_barrier(jnp.mean(center * center, -1, keepdims=True))
    return center * lax.rsqrt(spread + EPSILON) * scale_gain + offset

def matmul(left, right):
    return jnp.dot(left, right, precision=PRECISE)

def forward(inputs, params, segment):
    ln1_gain, ln1_bias, w_qkv, b_query, b_value, w_out, b_out, ln2_gain, ln2_bias, w_up, b_up, w_down, b_down = params
    row_count = inputs.shape[0]
    keep_rows = (segment >= 0).astype(jnp.float32)[:, None]
    normed = low(layer_norm(inputs, ln1_gain, ln1_bias))
    packed = matmul(normed, w_qkv)
    query_rows = low(low_back(packed[:, :D] + b_query)).reshape(row_count, HEADS, HEAD_DIM)
    key_rows = low(low_back(packed[:, D:2 * D])).reshape(row_count, HEADS, HEAD_DIM)
    value_rows = low(low_back(packed[:, 2 * D:] + b_value)).reshape(row_count, HEADS, HEAD_DIM)
    scores = jnp.einsum('qhd,khd->hqk', query_rows, key_rows, precision=PRECISE) * HEAD_DIM ** (-0.5)
    same_seq = segment[:, None] == segment[None, :]
    scores = low_back(jnp.where(same_seq[None], scores, NEGATIVE))
    weights = low(jax.nn.softmax(scores, axis=-1))
    mixed_rows = jnp.einsum('hqk,khd->qhd', weights, value_rows, precision=PRECISE).reshape(row_count, D)
    mixed_rows = low(low_back(mixed_rows))
    branch = low_back(matmul(mixed_rows, w_out) + b_out)
    middle = inputs + keep_rows * branch
    normed_two = low(layer_norm(middle, ln2_gain, ln2_bias))
    hidden = low_back(matmul(normed_two, w_up) + b_up)
    active = low(jax.nn.gelu(hidden))
    return middle + keep_rows * (matmul(active, w_down) + b_down)

def reference(tokens, segment, ln1_gain, ln1_bias, w_qkv, b_query, b_value, w_out, b_out, ln2_gain, ln2_bias, w_up, b_up, w_down, b_down, cotangent):
    params = tuple((part_arr.astype(jnp.float32) for part_arr in (ln1_gain, ln1_bias, w_qkv, b_query, b_value, w_out, b_out, ln2_gain, ln2_bias, w_up, b_up, w_down, b_down)))
    blocks = tokens.astype(jnp.float32).reshape(-1, ROWS_DEV, D)
    seg_blocks = segment.reshape(-1, ROWS_DEV)
    cot_blocks = cotangent.astype(jnp.float32).reshape(-1, ROWS_DEV, D)

    def one_block(totals, block):
        inputs, seg_rows, cot_rows = block
        result, pull_back = jax.vjp(lambda values_in, params_in: forward(values_in, params_in, seg_rows), inputs, params)
        grad_in, grad_params = pull_back(cot_rows)
        totals = jax.tree.map(jnp.add, totals, grad_params)
        return (totals, (result.astype(jnp.bfloat16), grad_in.astype(jnp.bfloat16)))
    start_totals = jax.tree.map(jnp.zeros_like, params)
    totals, (outputs, grads_in) = lax.scan(one_block, start_totals, (blocks, seg_blocks, cot_blocks))
    return (outputs.reshape(-1, D), grads_in.reshape(-1, D), totals[0], totals[1], totals[2], totals[3], totals[4], totals[5], totals[6], totals[7], totals[8], totals[9], totals[10], totals[11], totals[12])
```

```python
import functools

import jax
import jax.numpy as jnp
from jax import lax
from jax.experimental import pallas as pl
from jax.experimental.pallas import tpu as pltpu
from jax.sharding import PartitionSpec as P

HEADS = 12
EPSILON = 1e-06
LOG2E = 1.4426950408889634
BF = jnp.bfloat16
F32 = jnp.float32
RUNS = 6
SLICES = 4
SMALL = 256
WINDOW = 384
PAIRS = 6
BLANK = -8e9
NOTHING = 5e8
VMEM_BYTES = 28 * 1024 * 1024

IN_VMEM = pl.BlockSpec(memory_space=pltpu.VMEM)
IN_SMEM = pl.BlockSpec(memory_space=pltpu.SMEM)


def shape_of(shape, dtype):
    return jax.ShapeDtypeStruct(shape, dtype)


def params(**more):
    return pltpu.CompilerParams(vmem_limit_bytes=VMEM_BYTES, **more)


def cost(flops, moved, exps=0):
    return pl.CostEstimate(flops=int(flops), bytes_accessed=int(moved), transcendentals=int(exps))


def mm(left, right):
    return lax.dot_general(left, right, (((1,), (0,)), ((), ())), preferred_element_type=F32)


def mm_nt(left, right):
    return lax.dot_general(left, right, (((1,), (1,)), ((), ())), preferred_element_type=F32)


def chosen(mask, yes, no):
    return jnp.where(mask, yes.astype(F32), no.astype(F32)).astype(BF)


def turned(matrix):
    return jnp.transpose(matrix.astype(F32)).astype(BF)


def rows_below(base, size, limit):
    return base + lax.broadcasted_iota(jnp.int32, (size, 1), 0) < limit


def normalize(values):
    center = values - jnp.mean(values, -1, keepdims=True)
    spread = jnp.mean(center * center, -1, keepdims=True)
    inverse = lax.rsqrt(spread + EPSILON)
    return center * inverse, inverse


def kept_rows(counts):
    total = counts[0]
    for label in range(1, RUNS - 1):
        total = total + counts[label]
    return total


def chip_at(index, order):
    if order == "yxz":
        return (index & 3) * 4 + (index >> 3) * 2 + ((index >> 2) & 1)
    if order == "xyz":
        return (index & 3) * 4 + ((index >> 2) & 1) * 2 + (index >> 3)
    return index


def place_at(offset, order):
    if order == "yxz":
        return ((offset >> 1) & 1) * 8 + (offset & 1) * 4 + (offset >> 2)
    if order == "xyz":
        return (offset & 1) * 8 + ((offset >> 1) & 1) * 4 + (offset >> 2)
    return offset


def lay(source, chip, order, store):
    blocks, blk = source.shape[:2]
    for index in range(blocks):
        store(slice(index * blk, (index + 1) * blk), source[place_at(index ^ chip, order)])


def hand(values, at, target, half, chip, order):
    blk = target.shape[2]
    for index in range(values.shape[0] // blk):
        place = place_at((at // blk + index) ^ chip, order)
        target[half, place, :, : values.shape[1]] = values[index * blk : (index + 1) * blk]


def qkv_kernel(
    spot, x_ref, ta0, ta1, tb0, tb1, a1t_ref, q_ref, k_ref, v_ref, wq, wk, wv, wo, small_ref, first_s, second_s, *, orders
):
    core, chip = spot[0], spot[1]
    rows, width = x_ref.shape

    table = second_s
    lay(ta0, chip, orders[0], lambda here, value: _put(first_s, table, core, here, value, width))
    lay(ta1, chip, orders[0], lambda here, value: _put(first_s, table, 1 - core, here, value, width))
    wq[...] = first_s[0]
    wv[...] = first_s[1]
    small = jnp.transpose(table[0].astype(F32))
    small_ref[...] = small[: small_ref.shape[0], :]
    lay(tb0, chip, orders[1], lambda here, value: _put(first_s, None, core, here, value, width))
    lay(tb1, chip, orders[1], lambda here, value: _put(first_s, None, 1 - core, here, value, width))
    wk[...] = first_s[0]
    wo[...] = first_s[1]
    gain, bias = small_ref[0:1, :], small_ref[1:2, :]
    bias_query, bias_value = small_ref[2:3, :], small_ref[3:4, :]
    step = 256
    for at in range(0, rows, step):
        here = slice(at, at + step)
        normal, _ = normalize(x_ref[here, :].astype(F32))
        a1 = (normal * gain + bias).astype(BF)
        a1t_ref[:, here] = jnp.transpose(normal * gain + bias).astype(BF)
        q_ref[here, :] = (mm(a1, wq[...]) + bias_query).astype(BF)
        k_ref[here, :] = mm(a1, wk[...]).astype(BF)
        v_ref[here, :] = (mm(a1, wv[...]) + bias_value).astype(BF)


def _put(main, table, half, here, value, width):
    main[half, here, :] = value[:, :width]
    if table is not None:
        table[half, here, :] = value[:, width:]


def qkv_call(spot, x, ta, tb, orders):
    rows, width = x.shape
    act, weight = shape_of((rows, width), BF), shape_of((width, width), BF)
    return pl.pallas_call(
        functools.partial(qkv_kernel, orders=orders),
        out_shape=(shape_of((width, rows), BF),) + (act,) * 3 + (weight,) * 4 + (shape_of((16, width), F32),),
        in_specs=[IN_SMEM] + [IN_VMEM] * 5,
        out_specs=(IN_VMEM,) * 9,
        scratch_shapes=[pltpu.VMEM((2, width, width), BF), pltpu.VMEM((2, width, SMALL), BF)],
        compiler_params=params(),
        cost_estimate=cost(6 * rows * width * width, 16 * width * width),
        name="norm_qkv",
    )(spot, x, *ta, *tb)


def lane_of(size):
    return lax.broadcasted_iota(jnp.int32, (size, 128), 1)


def for_runs(counts, rows, visit):
    def body(run, start):
        size = counts[run]
        end = start + size
        base = (start // 16) * 16
        span = end - base

        def windowed(window):
            at = jnp.minimum(base, rows - window)
            visit(at, window, at, window, start, end, start, end, run)

        pl.when((size > 0) & (span <= 128))(lambda: windowed(128))
        pl.when((span > 128) & (span <= 256))(lambda: windowed(256))
        pl.when((span > 256) & (span <= WINDOW))(lambda: windowed(WINDOW))

        @pl.when(span > WINDOW)
        def _():
            def part(index, carry):
                low = base + index * 128
                at = jnp.minimum(low, rows - 128)
                visit(at, 128, 0, rows, jnp.maximum(low, start), end, start, end, RUNS + index)
                return carry

            lax.fori_loop(0, (span + 127) // 128, part, 0)

        return end

    lax.fori_loop(0, RUNS, body, 0)


def inside(base, size, low, high, axis=0):
    shape = (size, 128) if axis == 0 else (1, size)
    place = base + lax.broadcasted_iota(jnp.int32, shape, axis)
    return (place >= low) & (place < high)


def marked(q_two, k_two, k_ok, head):
    spare = 64 if head == 0 else 0
    q_lane, k_lane = lane_of(q_two.shape[0]), lane_of(k_two.shape[0])
    q_half = (q_lane < 64) if head == 0 else (q_lane >= 64)
    one = jnp.where(q_lane == spare, 1.0, 0.0)
    bias = jnp.where(k_ok, 0.0, BLANK)
    return chosen(q_half, q_two, one), chosen(k_lane == spare, bias, k_two)


def attend_kernel(counts, q_ref, k_ref, v_ref, o_ref, lse_ref, *, scale):
    rows, width = q_ref.shape
    factor = scale * LOG2E

    def visit(q_base, q_size, k_base, k_size, q_low, q_high, k_low, k_high, slot):
        q_at, k_at = pl.ds(pl.multiple_of(q_base, 16), q_size), pl.ds(pl.multiple_of(k_base, 16), k_size)
        q_ok, k_ok = inside(q_base, q_size, q_low, q_high), inside(k_base, k_size, k_low, k_high)
        q_row_ok = inside(q_base, q_size, q_low, q_high, 1)

        def group(index, carry):
            heads = []
            for pair in range(PAIRS):
                lanes = pl.ds(pl.multiple_of((index * PAIRS + pair) * 128, 128), 128)
                q_two, k_two = q_ref[q_at, lanes], k_ref[k_at, lanes]
                for head in range(2):
                    q_own, k_own = marked(q_two, k_two, k_ok, head)
                    heads.append(mm_nt(k_own, q_own))
            weights, totals = [], []
            for at, scores in enumerate(heads):
                top = jnp.max(scores, 0, keepdims=True)
                weight = jnp.exp2((scores - top) * factor)
                total = jnp.sum(weight, 0, keepdims=True)
                lse = jnp.where(q_row_ok, top * factor + jnp.log2(total), NOTHING)
                lse_ref[slot, index, at : at + 1, :q_size] = lse
                weights.append(weight.astype(BF))
                totals.append(1.0 / total)
            for pair in range(PAIRS):
                lanes = pl.ds(pl.multiple_of((index * PAIRS + pair) * 128, 128), 128)
                v_turned = turned(v_ref[k_at, lanes])
                mixed = []
                for head in range(2):
                    at = 2 * pair + head
                    mixed.append(mm(v_turned[head * 64 : head * 64 + 64], weights[at]) * totals[at])
                mixed = jnp.transpose(jnp.concatenate(mixed, 0))
                o_ref[q_at, lanes] = chosen(q_ok, mixed, o_ref[q_at, lanes])
            return carry

        lax.fori_loop(0, width // 128 // PAIRS, group, 0)

    for_runs(counts, rows, visit)


def attend_call(counts, q, k, v):
    rows, width = q.shape
    return pl.pallas_call(
        functools.partial(attend_kernel, scale=(width // HEADS) ** -0.5),
        out_shape=(shape_of((rows, width), BF), shape_of((RUNS + rows // 128, width // 128 // PAIRS, 16, WINDOW), F32)),
        in_specs=[IN_SMEM] + [IN_VMEM] * 3,
        out_specs=(IN_VMEM, IN_VMEM),
        compiler_params=params(),
        cost_estimate=cost(8 * rows * 256 * width, 8 * rows * width, HEADS * rows * 256),
        name="attend",
    )(counts, q, k, v)


def attend_back_kernel(
    counts, q_ref, k_ref, v_ref, g_ref, lse_ref, dq_ref, dk_ref, dv_ref, dk_sum, dv_sum, *, scale
):
    rows, width = q_ref.shape
    factor = scale * LOG2E

    def visit(q_base, q_size, k_base, k_size, q_low, q_high, k_low, k_high, slot):
        q_at, k_at = pl.ds(pl.multiple_of(q_base, 16), q_size), pl.ds(pl.multiple_of(k_base, 16), k_size)
        q_ok, k_ok = inside(q_base, q_size, q_low, q_high), inside(k_base, k_size, k_low, k_high)
        whole = q_size == k_size
        def group(index, carry):
            spans = [pl.ds(pl.multiple_of((index * PAIRS + pair) * 128, 128), 128) for pair in range(PAIRS)]
            g_lane, k_first = lane_of(q_size), lane_of(k_size) < 64
            scores, slopes = [], []
            for lanes in spans:
                q_two, k_two, v_two, g_two = q_ref[q_at, lanes], k_ref[k_at, lanes], v_ref[k_at, lanes], g_ref[q_at, lanes]
                for head in range(2):
                    q_own, k_own = marked(q_two, k_two, k_ok, head)
                    g_half = (g_lane < 64) if head == 0 else (g_lane >= 64)
                    scores.append(mm_nt(k_own, q_own))
                    slopes.append(mm_nt(v_two, jnp.where(g_half, g_two.astype(F32), 0.0).astype(BF)))
            probs = []
            for at in range(2 * PAIRS):
                lse = lse_ref[slot, index, at : at + 1, :q_size]
                prob = jnp.exp2(scores[at] * factor - lse)
                slope = prob * slopes[at]
                slopes[at] = (slope - prob * jnp.sum(slope, 0, keepdims=True)).astype(BF)
                probs.append(prob.astype(BF))
            for pair, lanes in enumerate(spans):
                two = (2 * pair, 2 * pair + 1)
                k_turned = turned(k_ref[k_at, lanes])
                dvs = [mm(probs[at], g_ref[q_at, lanes]) for at in two]
                dks = [mm(slopes[at], q_ref[q_at, lanes]) for at in two]
                dqs = [mm(k_turned[at % 2 * 64 : at % 2 * 64 + 64], slopes[at]) for at in two]
                dq = jnp.transpose(jnp.concatenate(dqs, 0)) * scale
                dq_ref[q_at, lanes] = chosen(q_ok, dq, dq_ref[q_at, lanes])
                dk, dv = jnp.where(k_first, dks[0], dks[1]) * scale, jnp.where(k_first, dvs[0], dvs[1])
                if whole:
                    dk_ref[k_at, lanes] = chosen(k_ok, dk, dk_ref[k_at, lanes])
                    dv_ref[k_at, lanes] = chosen(k_ok, dv, dv_ref[k_at, lanes])
                else:
                    begun = slot > RUNS
                    dk = dk + jnp.where(begun, dk_sum[:, lanes], 0.0)
                    dv = dv + jnp.where(begun, dv_sum[:, lanes], 0.0)
                    dk_sum[:, lanes] = dk
                    dv_sum[:, lanes] = dv
                    dk_ref[:, lanes] = chosen(k_ok, dk, dk_ref[:, lanes])
                    dv_ref[:, lanes] = chosen(k_ok, dv, dv_ref[:, lanes])
            return carry

        lax.fori_loop(0, width // 128 // PAIRS, group, 0)

    for_runs(counts, rows, visit)


def attend_back_call(counts, q, k, v, grad, lse):
    rows, width = q.shape
    act = shape_of((rows, width), BF)
    return pl.pallas_call(
        functools.partial(attend_back_kernel, scale=(width // HEADS) ** -0.5),
        out_shape=(act, act, act),
        in_specs=[IN_SMEM] + [IN_VMEM] * 5,
        out_specs=(IN_VMEM,) * 3,
        scratch_shapes=[pltpu.VMEM((rows, width), F32), pltpu.VMEM((rows, width), F32)],
        compiler_params=params(),
        cost_estimate=cost(20 * rows * 256 * width, 18 * rows * width, HEADS * rows * 256),
        name="attend_back",
    )(counts, q, k, v, grad, lse)


def out_kernel(counts, o_ref, x_ref, w_ref, small_ref, cot_ref, y_ref, a2_ref, a2t_ref, ot_ref, gm_ref):
    limit = kept_rows(counts)
    out_bias, gain, bias = small_ref[4:5, :], small_ref[5:6, :], small_ref[6:7, :]
    step = 256
    for at in range(0, o_ref.shape[0], step):
        here = slice(at, at + step)
        valid = rows_below(at, step, limit)
        gm_ref[here, :] = jnp.where(valid, cot_ref[here, :].astype(F32), 0.0).astype(BF)
        branch = mm(o_ref[here, :], w_ref[...]) + out_bias
        middle = x_ref[here, :].astype(F32) + jnp.where(valid, branch, 0.0)
        y_ref[here, :] = middle
        a2 = normalize(middle)[0] * gain + bias
        a2_ref[here, :] = a2.astype(BF)
        a2t_ref[:, here] = jnp.transpose(a2).astype(BF)
        ot_ref[:, here] = turned(o_ref[here, :])


def out_call(counts, mixed, x, weights, small, cot):
    rows, width = x.shape
    return pl.pallas_call(
        out_kernel,
        out_shape=(
            shape_of((rows, width), F32),
            shape_of((rows, width), BF),
            shape_of((width, rows), BF),
            shape_of((width, rows), BF),
            shape_of((rows, width), BF),
        ),
        in_specs=[IN_SMEM] + [IN_VMEM] * 5,
        out_specs=(IN_VMEM,) * 5,
        compiler_params=params(),
        cost_estimate=cost(2 * rows * width * width, 10 * rows * width),
        name="out_norm",
    )(counts, mixed, x, weights, small, cot)


def feed_kernel(
    counts, spot, a2_ref, a2t_ref, gm_ref, small_ref, out_in, w0, w1, *rest, index, first, last, orders
):
    if first:
        out_ref, down_ref, grads, sums_ref = rest[:4]
        held, act_t, du_s = rest[4:]
    else:
        down_in, out_ref, down_ref, grads, sums_ref = rest[:5]
        held, act_t, du_s = rest[5:]
    core, chip = spot[0], spot[1]
    other = 1 - core
    lay(w0, chip, orders[0], lambda here, value: _put(held, None, core, here, value, value.shape[1]))
    lay(w1, chip, orders[0], lambda here, value: _put(held, None, other, here, value, value.shape[1]))
    limit = kept_rows(counts)
    up_bias = small_ref[8 + index : 9 + index, :]
    rows, width = a2_ref.shape
    step = 256
    sums = jnp.zeros((1, width), F32)
    for at in range(0, rows, step):
        here = slice(at, at + step)
        valid = rows_below(at, step, limit)
        hidden = mm(a2_ref[here, :], held[0]) + up_bias
        square = hidden * hidden
        inner = 0.7978845608028654 * hidden * (1.0 + 0.044715 * square)
        bend = jnp.tanh(inner)
        half = 0.5 * (1.0 + bend)
        act = hidden * half
        act_t[:, here] = jnp.transpose(act).astype(BF)
        act = act.astype(BF)
        slope = half + 0.5 * hidden * (1.0 - bend * bend) * (0.7978845608028654 * (1.0 + 0.134145 * square))
        du = mm_nt(gm_ref[here, :], held[1]) * slope
        du_low = du.astype(BF)
        du_s[here, :] = du_low
        sums = sums + jnp.sum(du_low.astype(F32), 0, keepdims=True)
        result = out_in[here, :] + jnp.where(valid, mm(act, held[1]), 0.0)
        if last:
            result = result + jnp.where(valid, small_ref[7:8, :], 0.0)
        out_ref[here, :] = result.astype(out_ref.dtype)
        back = mm_nt(du_low, held[0])
        if not first:
            back = back + down_in[here, :]
        down_ref[here, :] = back
    sums_ref[...] = sums
    part = width // 2
    for at in range(0, width, part):
        hand(mm(a2t_ref[at : at + part, :], du_s[...]).astype(BF), at, grads, core, chip, orders[1])
        hand(mm(act_t[at : at + part, :], gm_ref[...]).astype(BF), at, grads, other, chip, orders[1])


def feed_call(counts, spot, a2, a2t, gm, small, out_in, down_in, weights, index, orders):
    rows, width = a2.shape
    blocks, blk = weights[0].shape[:2]
    first, last = down_in is None, index == SLICES - 1
    operands = [counts, spot, a2, a2t, gm, small, out_in, *weights] + ([] if first else [down_in])
    return pl.pallas_call(
        functools.partial(feed_kernel, index=index, first=first, last=last, orders=orders),
        out_shape=(
            shape_of((rows, width), BF if last else F32),
            shape_of((rows, width), F32),
            shape_of((2, blocks, blk, width), BF),
            shape_of((1, width), F32),
        ),
        in_specs=[IN_SMEM, IN_SMEM] + [IN_VMEM] * (7 if first else 8),
        out_specs=(IN_VMEM,) * 4,
        scratch_shapes=[
            pltpu.VMEM((2, width, width), BF),
            pltpu.VMEM((width, rows), BF),
            pltpu.VMEM((rows, width), BF),
        ],
        compiler_params=params(),
        cost_estimate=cost(12 * rows * width * width, 20 * rows * width, rows * width),
        name=f"feed_slice_{'abcdefgh'[index]}",
    )(*operands)


def mid_kernel(counts, spot, y_ref, down_ref, cot_ref, ot_ref, w_ref, small_ref, dy_ref, do_ref, grad, sums_ref, db_s, *, order):
    limit = kept_rows(counts)
    gain = small_ref[5:6, :]
    rows, width = y_ref.shape
    step = 256
    sums = [jnp.zeros((1, width), F32) for _ in range(4)]
    for at in range(0, rows, step):
        here = slice(at, at + step)
        valid = rows_below(at, step, limit)
        normal, inverse = normalize(y_ref[here, :])
        back = down_ref[here, :]
        scaled = back * gain
        one = jnp.mean(scaled, -1, keepdims=True)
        two = jnp.mean(scaled * normal, -1, keepdims=True)
        cot = cot_ref[here, :].astype(F32)
        dy = cot + inverse * (scaled - one - normal * two)
        dy_ref[here, :] = dy
        db = jnp.where(valid, dy, 0.0).astype(BF)
        db_s[here, :] = db
        do_ref[here, :] = mm_nt(db, w_ref[...]).astype(BF)
        sums[0] = sums[0] + jnp.sum(db.astype(F32), 0, keepdims=True)
        sums[1] = sums[1] + jnp.sum(back * normal, 0, keepdims=True)
        sums[2] = sums[2] + jnp.sum(back, 0, keepdims=True)
        sums[3] = sums[3] + jnp.sum(jnp.where(valid, cot, 0.0), 0, keepdims=True)
    for index, row in enumerate(sums):
        sums_ref[index : index + 1, :] = row
    part = width // 2
    for at in range(0, width, part):
        hand(mm(ot_ref[at : at + part, :], db_s[...]).astype(BF), at, grad, 0, spot[1], order)
    grad[0, :, :, width:] = jnp.zeros_like(grad[0, :, :, width:])


def mid_call(counts, spot, y, down, cot, mixed, weights, small, blocks, order):
    rows, width = y.shape
    return pl.pallas_call(
        functools.partial(mid_kernel, order=order),
        out_shape=(
            shape_of((rows, width), F32),
            shape_of((rows, width), BF),
            shape_of((1, blocks, width // blocks, width + SMALL), BF),
            shape_of((4, width), F32),
        ),
        in_specs=[IN_SMEM, IN_SMEM] + [IN_VMEM] * 6,
        out_specs=(IN_VMEM,) * 4,
        scratch_shapes=[pltpu.VMEM((rows, width), BF)],
        compiler_params=params(),
        cost_estimate=cost(4 * rows * width * width, 18 * rows * width),
        name="mid_back",
    )(counts, spot, y, down, cot, mixed, weights, small)


def end_kernel(
    spot, x_ref, dy_ref, a1t_ref, dq_ref, dk_ref, dv_ref, wq, wk, wv, small_ref, mid_ref, up_ref, out_grad,
    tokens_ref, ga, gb, table_s, *, orders
):
    core, chip = spot[0], spot[1]
    other = 1 - core
    rows, width = x_ref.shape
    gb[other] = out_grad[0]
    part = width // 2
    for at in range(0, width, part):
        a1t = a1t_ref[at : at + part, :]
        hand(mm(a1t, dq_ref[...]).astype(BF), at, ga, core, chip, orders[0])
        hand(mm(a1t, dv_ref[...]).astype(BF), at, ga, other, chip, orders[0])
        hand(mm(a1t, dk_ref[...]).astype(BF), at, gb, core, chip, orders[1])
    gain = small_ref[0:1, :]
    sums = [jnp.zeros((1, width), F32) for _ in range(4)]
    step = 256
    for at in range(0, rows, step):
        here = slice(at, at + step)
        dq, dk, dv = dq_ref[here, :], dk_ref[here, :], dv_ref[here, :]
        back = mm_nt(dq, wq[...]) + mm_nt(dk, wk[...]) + mm_nt(dv, wv[...])
        normal, inverse = normalize(x_ref[here, :].astype(F32))
        scaled = back * gain
        one = jnp.mean(scaled, -1, keepdims=True)
        two = jnp.mean(scaled * normal, -1, keepdims=True)
        tokens_ref[here, :] = (dy_ref[here, :] + inverse * (scaled - one - normal * two)).astype(BF)
        sums[0] = sums[0] + jnp.sum(back * normal, 0, keepdims=True)
        sums[1] = sums[1] + jnp.sum(back, 0, keepdims=True)
        sums[2] = sums[2] + jnp.sum(dq.astype(F32), 0, keepdims=True)
        sums[3] = sums[3] + jnp.sum(dv.astype(F32), 0, keepdims=True)
    table_s[...] = jnp.zeros_like(table_s)
    for index in range(4):
        table_s[index : index + 1, :] = sums[index]
        table_s[4 + index : 5 + index, :] = mid_ref[index : index + 1, :]
        table_s[8 + index : 9 + index, :] = up_ref[index : index + 1, :]
    table = jnp.transpose(table_s[...]).astype(BF)
    blk = gb.shape[2]
    for index in range(width // blk):
        gb[core, place_at(index ^ chip, orders[1]), :, width:] = table[index * blk : (index + 1) * blk]


def end_call(spot, x, dy, a1, dq, dk, dv, wq, wk, wv, small, mid, ups, out_grad, orders):
    rows, width = x.shape
    blocks, blk = out_grad.shape[1:3]
    return pl.pallas_call(
        functools.partial(end_kernel, orders=orders),
        out_shape=(
            shape_of((rows, width), BF),
            shape_of((2, blocks, blk, width), BF),
            shape_of((2, blocks, blk, width + SMALL), BF),
        ),
        in_specs=[IN_SMEM] + [IN_VMEM] * 13,
        out_specs=(IN_VMEM,) * 3,
        scratch_shapes=[pltpu.VMEM((SMALL, width), F32)],
        compiler_params=params(),
        cost_estimate=cost(12 * rows * width * width, 18 * rows * width),
        name="qkv_norm_back",
    )(spot, x, dy, a1, dq, dk, dv, wq, wk, wv, small, mid, ups, out_grad)


def assemble(own, oth, spot, order):
    core, chip = spot[0], spot[1]
    blocks, blk, W = own.shape
    idx = jnp.array([place_at(a, order) for a in range(blocks)])
    pos = idx[jnp.arange(blocks) ^ chip]
    o, t = own[pos].reshape(-1, W), oth[pos].reshape(-1, W)
    return jnp.where(core == 0, o, t), jnp.where(core == 0, t, o)


def scatter_form(zero, one, spot, order, blocks):
    core, chip = spot[0], spot[1]
    W = zero.shape[1]
    src = jnp.array([chip_at(p, order) for p in range(blocks)]) ^ chip
    z, o = zero.reshape(blocks, -1, W)[src], one.reshape(blocks, -1, W)[src]
    return jnp.where(core == 0, jnp.stack([z, o]), jnp.stack([o, z]))


def x_qkv_call(spot, x, ta, tb, orders):
    width = x.shape[1]
    a0, a1w = assemble(ta[0], ta[1], spot, orders[0])
    wk, wo = assemble(tb[0], tb[1], spot, orders[1])
    wq, wv = a0[:, :width], a1w[:, :width]
    small = a0[:, width:].astype(F32).T[:16]
    n, _ = normalize(x.astype(F32))
    a1 = (n * small[0:1] + small[1:2]).astype(BF)
    return (a1.T, (mm(a1, wq) + small[2:3]).astype(BF), mm(a1, wk).astype(BF), (mm(a1, wv) + small[3:4]).astype(BF), wq, wk, wv, wo, small)


def x_out_call(counts, mixed, x, weights, small, cot):
    valid = rows_below(0, x.shape[0], kept_rows(counts))
    gm = jnp.where(valid, cot, 0).astype(BF)
    y = x.astype(F32) + jnp.where(valid, mm(mixed, weights) + small[4:5], 0.0)
    a2 = (normalize(y)[0] * small[5:6] + small[6:7]).astype(BF)
    return y, a2, a2.T, mixed.T, gm


def x_feed_call(counts, spot, a2, a2t, gm, small, out_in, down_in, weights, index, orders):
    wu, wd = assemble(weights[0], weights[1], spot, orders[0])
    valid = rows_below(0, a2.shape[0], kept_rows(counts))
    h = mm(a2, wu) + small[8 + index : 9 + index]
    act, pull = jax.vjp(jax.nn.gelu, h)
    act = act.astype(BF)
    du = pull(mm_nt(gm, wd))[0].astype(BF)
    out = out_in + jnp.where(valid, mm(act, wd), 0.0)
    last = index == SLICES - 1
    if last:
        out = (out + jnp.where(valid, small[7:8], 0.0)).astype(BF)
    back = mm_nt(du, wu) + (0 if down_in is None else down_in)
    g = scatter_form(mm(a2t, du).astype(BF), mm(act.T, gm).astype(BF), spot, orders[1], weights[0].shape[0])
    return out, back, g, jnp.sum(du.astype(F32), 0, keepdims=True)


def x_mid_call(counts, spot, y, down, cot, mixed, weights, small, blocks, order):
    valid = rows_below(0, y.shape[0], kept_rows(counts))
    n, inv = normalize(y)
    c = down * small[5:6]
    dy = cot.astype(F32) + inv * (c - jnp.mean(c, -1, keepdims=True) - n * jnp.mean(c * n, -1, keepdims=True))
    db = jnp.where(valid, dy, 0.0).astype(BF)
    do = mm_nt(db, weights).astype(BF)
    s = jnp.stack([jnp.sum(db.astype(F32), 0), jnp.sum(down * n, 0), jnp.sum(down, 0), jnp.sum(jnp.where(valid, cot.astype(F32), 0.0), 0)])
    g = jnp.pad(mm(mixed, db).astype(BF), ((0, 0), (0, SMALL)))
    core, chip = spot[0], spot[1]
    src = jnp.array([chip_at(p, order) for p in range(blocks)]) ^ chip
    return dy, do, g.reshape(blocks, -1, g.shape[1])[src][None], s


def x_end_call(spot, x, dy, a1, dq, dk, dv, wq, wk, wv, small, mid, ups, out_grad, orders):
    blocks = out_grad.shape[1]
    back = mm_nt(dq, wq) + mm_nt(dk, wk) + mm_nt(dv, wv)
    n, inv = normalize(x.astype(F32))
    c = back * small[0:1]
    tok = (dy + inv * (c - jnp.mean(c, -1, keepdims=True) - n * jnp.mean(c * n, -1, keepdims=True))).astype(BF)
    ga = scatter_form(mm(a1, dq).astype(BF), mm(a1, dv).astype(BF), spot, orders[0], blocks)
    sums = jnp.stack([jnp.sum(back * n, 0), jnp.sum(back, 0), jnp.sum(dq.astype(F32), 0), jnp.sum(dv.astype(F32), 0)])
    table = jnp.concatenate([sums, mid, ups, jnp.zeros((SMALL - 12, x.shape[1]), F32)], 0).T.astype(BF)
    gk = jnp.concatenate([mm(a1, dk).astype(BF), table], 1)
    gkb = scatter_form(gk, gk, spot, orders[1], blocks)[0]
    return tok, ga, jnp.where(spot[0] == 0, jnp.stack([gkb, out_grad[0]]), jnp.stack([out_grad[0], gkb]))


def columns(vectors):
    table = jnp.stack(vectors, 1)
    return jnp.pad(table, ((0, 0), (0, SMALL - table.shape[1])))


def flip(value, bit):
    return lax.ppermute(value, "dp", [(at, at ^ bit) for at in range(lax.axis_size("dp"))])


def pick(core, zero, one):
    return jnp.where(core == 0, zero, one)


class Staged:
    def __init__(self):
        place = lax.axis_index("dp")
        self.core = place % 2
        self.spot = jnp.stack([place % 2, place // 2]).astype(jnp.int32)
        self.blocks = lax.axis_size("dp") // 2

    def gather_order(self, index):
        return ("yxz", "xyz")[index % 2]

    def scatter_order(self, index):
        return ("xyz", "yxz")[index % 2]

    def gather(self, vectors, b_up, w_qkv, w_out, w_up, w_down):
        core = self.core
        own_rows, width = w_out.shape
        devices = width // own_rows
        ups = w_up.reshape(own_rows, devices, SLICES, own_rows).transpose(2, 0, 1, 3).reshape(SLICES, own_rows, width)
        downs = w_down.reshape(SLICES, own_rows, width)
        extra = columns(vectors + [b_up.reshape(SLICES, own_rows)[at] for at in range(SLICES)])
        zero = jnp.concatenate([w_qkv[:, :width], extra, w_qkv[:, width : 2 * width], *ups], 1)
        one = jnp.concatenate([w_qkv[:, 2 * width :], extra, w_out, *downs], 1)
        sent = pick(core, one, zero)
        kept = pick(core, zero, one)
        came = flip(sent, 1)
        both = jnp.concatenate([pick(core, kept, came), pick(core, came, kept)], 0)
        edges = [0, width + SMALL] + [width * at + SMALL for at in range(2, SLICES + 3)]
        results = []
        for index in range(SLICES + 2):
            piece = both[:, edges[index] : edges[index + 1]]
            held = jnp.stack([piece, flip(piece, 8), flip(piece, 16), flip(piece, 24)])
            for bit in ((2, 4), (4, 2))[index % 2]:
                held = jnp.concatenate([held, flip(held, bit)], 0)
            results.append((held, flip(held, 1)))
        return results

    def reduce(self, index, parts):
        def add(left, right):
            return (left.astype(F32) + right.astype(F32)).astype(BF)

        came = flip(parts[1], 1)
        held = parts[0]
        for bit in ((2, 4), (4, 2))[index % 2]:
            half = held.shape[0] // 2
            sent, held = add(held[half:], came[half:]), add(held[:half], came[:half])
            came = flip(sent, bit)
        pieces = [add(held[at], came[at]) for at in range(1, 4)]
        total = held[0].astype(F32) + came[0].astype(F32)
        for at in range(1, 4):
            total = total + flip(pieces[at - 1], 8 * at).astype(F32)
        half = total.shape[0] // 2
        kept = pick(self.core, total[:half], total[half:])
        came = flip(pick(self.core, total[half:], total[:half]), 1)
        return pick(self.core, kept, came), pick(self.core, came, kept)

    def finish(self, reduced):
        (q, v), (k_small, out) = reduced[0], reduced[1]
        width = q.shape[1]
        own_rows = q.shape[0]
        k, small = k_small[:, :width], k_small[:, width:]
        ups = jnp.stack([pair[0] for pair in reduced[2:]])
        devices = width // own_rows
        up = ups.reshape(SLICES, own_rows, devices, own_rows).transpose(1, 2, 0, 3).reshape(own_rows, SLICES * width)
        down = jnp.concatenate([pair[1] for pair in reduced[2:]], 0)
        vectors = [small[:, at] for at in range(8)]
        b_up = small[:, 8 : 8 + SLICES].T.reshape(-1)
        return vectors, b_up, jnp.concatenate([q, k, v], 1), out[:, :width], up, down


class Plain:
    def __init__(self):
        self.spot = jnp.zeros((2,), jnp.int32)
        self.blocks = 16

    def gather_order(self, index):
        return None

    def scatter_order(self, index):
        return None

    def gather(self, vectors, b_up, w_qkv, w_out, w_up, w_down):
        def whole(value):
            return lax.all_gather(value, "dp", axis=0, tiled=True)

        w_qkv, w_out, w_up, w_down, b_up = whole(w_qkv), whole(w_out), whole(w_up), whole(w_down), whole(b_up)
        width = w_out.shape[0]
        extra = columns([whole(vector) for vector in vectors] + list(b_up.reshape(SLICES, width)))
        pairs = [
            (jnp.concatenate([w_qkv[:, :width], extra], 1), jnp.concatenate([w_qkv[:, 2 * width :], extra], 1)),
            (w_qkv[:, width : 2 * width], w_out),
        ]
        for at in range(SLICES):
            here = slice(at * width, (at + 1) * width)
            pairs.append((w_up[:, here], w_down[here]))
        return [tuple(one.reshape(self.blocks, -1, one.shape[1]) for one in pair) for pair in pairs]

    def reduce(self, index, parts):
        return parts.reshape(2, -1, parts.shape[-1]).astype(F32)

    def finish(self, reduced):
        def owned(value):
            return lax.psum_scatter(value, "dp", scatter_dimension=0, tiled=True)

        width = reduced[0].shape[-1]
        small = reduced[1][0][:, width:].T
        up = jnp.concatenate([pair[0] for pair in reduced[2:]], 1)
        down = jnp.concatenate([pair[1] for pair in reduced[2:]], 0)
        qkv = jnp.concatenate([reduced[0][0], reduced[1][0][:, :width], reduced[0][1]], 1)
        vectors = [owned(small[at]) for at in range(8)]
        b_up = owned(small[8 : 8 + SLICES].reshape(-1))
        return vectors, b_up, owned(qkv), owned(reduced[1][1][:, :width]), owned(up), owned(down)


def local(
    tokens, segment, ln1_gain, ln1_bias, w_qkv, b_query, b_value, w_out, b_out, ln2_gain, ln2_bias,
    w_up, b_up, w_down, b_down, cotangent,
):
    plan = Staged() if lax.axis_size("dp") == 32 else Plain()
    vectors = [ln1_gain, ln1_bias, b_query, b_value, b_out, ln2_gain, ln2_bias, b_down]
    weights = plan.gather(vectors, b_up, w_qkv, w_out, w_up, w_down)
    spot = plan.spot
    labels = jnp.array(list(range(RUNS - 1)) + [-1], jnp.int32)
    counts = jnp.sum((segment[None, :] == labels[:, None]).astype(jnp.int32), 1)
    gathered = [plan.gather_order(at) for at in range(SLICES + 2)]
    scattered = [plan.scatter_order(at) for at in range(SLICES + 2)]

    a1t, q, k, v, wq, wk, wv, wo, small = qkv_call(spot, tokens, weights[0], weights[1], gathered[:2])
    mixed, lse = attend_call(counts, q, k, v)
    middle, a2, a2t, mixed_t, gm = out_call(counts, mixed, tokens, wo, small, cotangent)
    result, down = middle, None
    up_sums, reduced = [], [None] * (SLICES + 2)
    for at in range(SLICES):
        orders = (gathered[2 + at], scattered[2 + at])
        result, down, grads, sums = x_feed_call(
            counts, spot, a2, a2t, gm, small, result, down, weights[2 + at], at, orders
        )
        up_sums.append(sums)
        reduced[2 + at] = plan.reduce(2 + at, grads)
    dy, d_mixed, grad_out, mid_sums = x_mid_call(
        counts, spot, middle, down, cotangent, mixed_t, wo, small, plan.blocks, scattered[1]
    )
    dq, dk, dv = attend_back_call(counts, q, k, v, d_mixed, lse)
    grad_tokens, grad_a, grad_b = x_end_call(
        spot, tokens, dy, a1t, dq, dk, dv, wq, wk, wv, small, mid_sums, jnp.concatenate(up_sums, 0), grad_out,
        scattered[:2],
    )
    reduced[0] = plan.reduce(0, grad_a)
    reduced[1] = plan.reduce(1, grad_b)
    vectors, grad_b_up, grad_qkv, grad_w_out, grad_up, grad_down = plan.finish(reduced)
    gain_one, bias_one, grad_query, grad_value, grad_out_bias, gain_two, bias_two, grad_down_bias = vectors
    return (
        result, grad_tokens, gain_one, bias_one, grad_qkv, grad_query, grad_value, grad_w_out, grad_out_bias,
        gain_two, bias_two, grad_up, grad_b_up, grad_down, grad_down_bias,
    )


def solution(mesh):
    matrix, vector = P("dp", None), P("dp")
    return jax.shard_map(
        local,
        mesh=mesh,
        in_specs=(
            matrix, vector, vector, vector, matrix, vector, vector, matrix, vector, vector, vector,
            matrix, vector, matrix, vector, matrix,
        ),
        out_specs=(
            matrix, matrix, vector, vector, matrix, vector, vector, matrix, vector, vector, vector,
            matrix, vector, matrix, vector,
        ),
        check_vma=False,
    )
```
